256 devices in a mesh: ctx: 16 (over x_hi, z), head: 8 (over y, core), pair: 2 (over x_lo).
Axes of the slice: x: 4 (x_hi: 2, x_lo: 2; x = x_hi * 2 + x_lo), y: 4, z: 8, core: 2. Of those that a mesh axis runs over, the one named last changes fastest.
Arguments:
- queries: bfloat16 [2048, 64, 128], P(('pair', 'ctx'), 'head'), parts along dimension 0, may hold values from -6 to 6
- keys: bfloat16 [65536, 8, 128], P(('pair', 'ctx'), 'head'), parts along dimension 0, may hold values from -6 to 6
- values: bfloat16 [65536, 8, 128], P(('pair', 'ctx'), 'head'), parts along dimension 0, may hold values from -6 to 6
- lengths: int32 [4], P('pair'), parts along dimension 0, may hold values from 256 to 512, as said below
- prompt_lengths: int32 [2], P('pair'), parts along dimension 0, may hold values from 16384 to 32768
- out_weight: bfloat16 [8192, 8192], P('head', 'ctx'), may hold values from -0.0625 to 0.0625
Outputs:
- projected: float32 [2048, 8192], P(('pair', 'head'), 'ctx'), parts along dimension 0
The draws below stay inside these ranges and needn't reach their ends.
There are 2 independent parts, one for each index of `pair`. The reference program is written for one: setup_inputs(seed, part) draws one part's arguments, and reference() takes and returns one part's arrays. A program takes and returns all parts, laid end to end along the dimension named above; an argument that names none is the same for every part. Nothing has to cross between parts.
Inputs may be any that keep to these rules, and one draw needn't show every extreme that they name: `lengths`: one of the two responses has exactly 512 real tokens, the other at least 256.
All inputs are finite; a program needn't handle non-finite values.
Results may differ from the reference program's by a relative error of at most 0.013.
Values may be sent and summed in bfloat16 or wider, within the bound.
A program may use at most 64 MiB of HBM per device.

```python
import jax
import jax.numpy as jnp
from jax import lax

D = 8192
QUERY_HEADS = 64
KEY_VALUE_HEADS = 8
HEAD_WIDTH = 128
RESP = 512
GROUP = 8
QTOK = 1024
CONTEXT_SPAN = 32768


def draw_queries(key, part):
    key = jax.random.fold_in(key, 11)
    attended_output = jnp.clip(jax.random.normal(key, (QTOK, QUERY_HEADS, HEAD_WIDTH), jnp.float32), -6.0, 6.0)
    return attended_output.astype(jnp.bfloat16)


def draw_keys(key, part):
    key = jax.random.fold_in(key, 23)
    attended_output = jnp.clip(jax.random.normal(key, (CONTEXT_SPAN, KEY_VALUE_HEADS, HEAD_WIDTH), jnp.float32), -6.0, 6.0)
    return attended_output.astype(jnp.bfloat16)


def draw_lengths(key, part):
    key = jax.random.fold_in(key, 5)
    leading_key, second_key = jax.random.split(key)
    drawn = jax.random.randint(leading_key, (2,), RESP // 2, RESP + 1)
    longest = jax.random.randint(second_key, (), 0, 2)
    return jnp.where(jnp.arange(2) == longest, RESP, drawn).astype(jnp.int32)


def shard_levels(rng, extent, pieces, least, largest):
    level, own = 1.0, jax.random.fold_in(rng, 6)
    for axis_at, shards_of in pieces:
        heights = jnp.exp(jax.random.uniform(jax.random.fold_in(own, axis_at), (shards_of,), jnp.float32, least / len(pieces), largest / len(pieces)))
        level = level * jnp.repeat(heights, extent[axis_at] // shards_of).reshape([-1 if axis == axis_at else 1 for axis in range(len(extent))])
    return level


def noise(stream_key, extent, scale, limit, pieces=(), held_as=jnp.bfloat16):
    gain = shard_levels(stream_key, extent, pieces, -0.22, 0.18) if pieces else 1.0
    values = jax.random.normal(stream_key, extent, jnp.float32) * scale * gain
    return jnp.minimum(jnp.maximum(values, -limit), limit).astype(held_as)


def setup_inputs(seed: int = 0, part: int = 0) -> dict:
    key_list = jax.random.split(jax.random.key(seed), 7)
    part_splits = jax.random.split(jax.random.fold_in(key_list[6], part), 7)
    return {
        "queries": draw_queries(jax.random.fold_in(jax.random.fold_in(key_list[6], part), 71), part),
        "keys": draw_keys(jax.random.fold_in(jax.random.fold_in(key_list[6], part), 71), part),
        "values": noise(part_splits[2], (CONTEXT_SPAN, KEY_VALUE_HEADS, HEAD_WIDTH), 1.0, 6.0, ((0, 16), (1, 8))),
        "lengths": draw_lengths(jax.random.fold_in(jax.random.fold_in(key_list[6], part), 71), part),
        "prompt_lengths": jax.random.randint(part_splits[4], (1,), CONTEXT_SPAN // 2, CONTEXT_SPAN + 1).astype(jnp.int32),
        "out_weight": noise(key_list[5], (QUERY_HEADS * HEAD_WIDTH, D), (QUERY_HEADS * HEAD_WIDTH) ** -0.5, 0.0625, ((0, 8), (1, 16))),
    }


masked_score = -1.0e30


def reference(queries, keys, values, lengths, prompt_lengths, out_weight):
    score_scale = HEAD_WIDTH ** -0.5
    row_ids = jnp.arange(QTOK, dtype=jnp.int32)
    response_id = row_ids // RESP
    local_pos = row_ids % RESP
    is_live = local_pos < jnp.where(response_id == 0, lengths[0], lengths[1])
    key_pos = jnp.arange(CONTEXT_SPAN, dtype=jnp.int32)
    visible = jnp.broadcast_to((key_pos < prompt_lengths[0])[None, :], (QTOK, CONTEXT_SPAN))

    def one_head(head_index):
        query_head = lax.dynamic_index_in_dim(queries, head_index, 1, keepdims=False)
        key_head = lax.dynamic_index_in_dim(keys, head_index // GROUP, 1, keepdims=False)
        value_head = lax.dynamic_index_in_dim(values, head_index // GROUP, 1, keepdims=False)
        scores = jnp.dot(query_head, key_head.T, preferred_element_type=jnp.float32) * score_scale
        scores = jnp.where(visible, scores, masked_score)
        peak = jnp.max(scores, axis=1)
        weights = jnp.where(visible, jnp.exp(scores - peak[:, None]), 0.0)
        total = jnp.sum(weights, axis=1)
        mixed = jnp.dot(weights.astype(jnp.bfloat16), value_head, preferred_element_type=jnp.float32)
        mixed = mixed / total[:, None]
        mixed = jnp.where(is_live[:, None], mixed, 0.0)
        return mixed.astype(jnp.bfloat16)

    heads_out = lax.map(one_head, jnp.arange(QUERY_HEADS, dtype=jnp.int32))
    mixed = jnp.transpose(heads_out, (1, 0, 2)).reshape(QTOK, QUERY_HEADS * HEAD_WIDTH)
    return jnp.dot(mixed, out_weight, preferred_element_type=jnp.float32)
```

```python
import functools

import jax
import jax.numpy as jnp
from jax import lax
from jax.experimental import pallas as pl
from jax.experimental.pallas import tpu as pltpu
from jax.sharding import PartitionSpec as P

MESH = pl.DeviceIdType.MESH
F32 = jnp.float32
BF16 = jnp.bfloat16
NT = (((1,), (1,)), ((), ()))
NN = (((1,), (0,)), ((), ()))
HIDDEN = -1e30
LOG2E = 1.4426950408889634

TOKENS = 64
GROUP = 8
WIDTH = 128
ROWS = TOKENS * GROUP
SPAN = 1024
STRIP = 256
HALF = ROWS // 2
RING = 8
FEATURES = GROUP * WIDTH
COLUMNS = 512
SCALE = WIDTH ** -0.5 * LOG2E


def kernel(
    q_ref, k_ref, v_ref, len_ref, plen_ref, w_ref, out_ref,
    q_all, k_all, vt_all, score, peak, acc, top,
    go_o, go_s, in_o, in_s, turn, mixed, part, mate_in, y_out, y_in, own,
    kv_send, kv_recv, q_send, q_recv, rs_send, rs_recv, rt_send, rt_recv,
    mx_send, mx_recv, ag_send, ag_recv, co_send, co_recv, y_send, y_recv,
):
    ctx = lax.axis_index("ctx")
    head = lax.axis_index("head")
    side, z = ctx // RING, ctx % RING
    y, core = head // 2, head % 2

    def z_at(step):
        return {"ctx": side * RING + (z + step + RING) % RING}

    def y_at(to):
        return {"head": to * 2 + core}

    partner = {"ctx": (1 - side) * RING + z}
    mate = {"head": y * 2 + 1 - core}

    def remote(src, dst, send, recv, to):
        return pltpu.make_async_remote_copy(
            src_ref=src, dst_ref=dst, send_sem=send, recv_sem=recv,
            device_id=to, device_id_type=MESH,
        )

    barrier = pltpu.get_barrier_semaphore()
    for to in (z_at(1), z_at(-1), partner, mate, y_at((y + 1) % 4), y_at((y + 2) % 4), y_at((y + 3) % 4)):
        pl.semaphore_signal(barrier, inc=1, device_id=to, device_id_type=MESH)

    plen = plen_ref[0]

    def chunk_start(chunk):
        holder = jnp.where(chunk < 2, side, 1 - side)
        return (holder * RING + z) * 2 * SPAN + (chunk % 2) * SPAN

    q_all[0] = q_ref[...]
    for chunk in range(2):
        start = chunk_start(chunk)
        rows = pl.ds(chunk * SPAN, SPAN)
        keys = k_ref[rows, :].astype(F32)
        seen = start + lax.broadcasted_iota(jnp.int32, (SPAN, WIDTH), 0) < plen
        k_all[chunk] = jnp.where(seen, keys, keys[0:1, :]).astype(BF16)
        vals = jnp.where(seen, v_ref[rows, :].astype(F32), 0.0)
        vt_all[chunk, 0:WIDTH, :] = vals.T.astype(BF16)
    for chunk in range(4):
        seen = chunk_start(chunk) + lax.broadcasted_iota(jnp.int32, (16, SPAN), 1) < plen
        vt_all[chunk, WIDTH:, :] = jnp.where(seen, 1.0, 0.0).astype(BF16)
    acc[...] = jnp.zeros_like(acc)
    top[...] = jnp.full_like(top, HIDDEN)

    def q_copy(n, half, slot):
        to = jnp.where(slot % 2 == 1, 1, -1)
        rows = pl.ds(half * HALF, HALF)
        return remote(
            q_all.at[n, rows], q_all.at[slot, rows],
            q_send.at[slot * 2 + half], q_recv.at[slot * 2 + half], z_at(to),
        )

    def kv_copy(index):
        chunk = index // 2
        if index % 2 == 0:
            src, dst = k_all.at[chunk], k_all.at[chunk + 2]
        else:
            src, dst = vt_all.at[chunk, 0:WIDTH], vt_all.at[chunk + 2, 0:WIDTH]
        return remote(src, dst, kv_send.at[index], kv_recv.at[index], partner)

    pl.semaphore_wait(barrier, 7)
    for half in range(2):
        for slot in (1, 2):
            q_copy(0, half, slot).start()
    for index in range(4):
        kv_copy(index).start()

    def task(t):
        n = jnp.where(t < 16, t // 2, jnp.where(t < 24, t - 16, 31 - t))
        chunk = jnp.where(t < 16, t % 2, jnp.where(t < 24, 2, 3))
        return n, chunk

    def ready(t):
        @pl.when(jnp.logical_and(jnp.logical_and(t >= 2, t < 16), t % 2 == 0))
        def _():
            n = t // 2
            for half in range(2):
                q_copy(0, half, n).wait_recv()

                @pl.when(n + 2 < RING)
                def _():
                    q_copy(n, half, n + 2).start()

        @pl.when(t == 16)
        def _():
            kv_copy(0).wait_recv()
            kv_copy(1).wait_recv()

        @pl.when(t == 24)
        def _():
            kv_copy(2).wait_recv()
            kv_copy(3).wait_recv()

    def step(ahead, slot_ahead, now, slot_now):
        if ahead is not None:
            n_ahead, c_ahead = task(ahead)
            queries = q_all[n_ahead]
        if now is not None:
            n_now, c_now = task(now)
            best = peak[slot_now, 0:1, :]
        total = highest = None
        for strip in range(0, SPAN, STRIP):
            at = pl.ds(strip, STRIP)
            if ahead is not None:
                s = lax.dot_general(k_all[c_ahead, at, :], queries, NT, preferred_element_type=F32)
                score[slot_ahead, at, :] = s
                high = jnp.max(s.reshape(STRIP // 8, 8, ROWS), axis=0)
                highest = high if highest is None else jnp.maximum(highest, high)
            if now is not None:
                weights = jnp.exp2((score[slot_now, at, :] - best) * SCALE).astype(BF16)
                term = lax.dot_general(vt_all[c_now, :, at], weights, NN, preferred_element_type=F32)
                total = term if total is None else total + term
        if ahead is not None:
            peak[slot_ahead, 0:1, :] = jnp.max(highest, axis=0, keepdims=True)
        if now is not None:
            best = jnp.where(chunk_start(c_now) < plen, best, HIDDEN)
            old = top[n_now, 0:1, :]
            new = jnp.maximum(old, best)
            top[n_now, 0:1, :] = new
            acc[n_now] = acc[n_now] * jnp.exp2((old - new) * SCALE) + total[0:136] * jnp.exp2((best - new) * SCALE)

    def rs_copies(n, half):
        to = jnp.where(n % 2 == 1, -1, 1)
        lanes = pl.ds(half * HALF, HALF)
        i = n * 2 + half
        return (
            remote(go_o.at[i], in_o.at[i], rs_send.at[i], rs_recv.at[i], z_at(to)),
            remote(go_s.at[i], in_s.at[i], rt_send.at[i], rt_recv.at[i], z_at(to)),
        )

    def join(n, half, source):
        for copy in rs_copies(source, half):
            copy.wait_recv()
        lanes = pl.ds(half * HALF, HALF)
        i = source * 2 + half
        old, best = top[n, 0:1, lanes], in_s[i, 0:1, :]
        new = jnp.maximum(old, best)
        keep, add = jnp.exp2((old - new) * SCALE), jnp.exp2((best - new) * SCALE)
        top[n, 0:1, lanes] = new
        acc[n, 0:WIDTH, lanes] = acc[n, 0:WIDTH, lanes] * keep + in_o[i].astype(F32) * add
        acc[n, WIDTH:, lanes] = acc[n, WIDTH:, lanes] * keep + in_s[i, 8:16, :] * add

    def pass_on(t):
        n = 31 - t
        for half in range(2):
            lanes = pl.ds(half * HALF, HALF)

            @pl.when(jnp.logical_and(t >= 24, n + 2 < RING))
            def _():
                join(n, half, n + 2)

            @pl.when(jnp.logical_and(t >= 24, n >= 1))
            def _():
                i = n * 2 + half
                go_o[i] = acc[n, 0:WIDTH, lanes].astype(BF16)
                go_s[i, 0:8, :] = top[n, :, lanes]
                go_s[i, 8:16, :] = acc[n, WIDTH:, lanes]
                for copy in rs_copies(n, half):
                    copy.start()

    ready(0)
    step(0, 0, None, None)

    def two(g, _):
        t = g * 2
        ready(t + 1)
        step(t + 1, 1, t, 0)
        pass_on(t)
        ready(t + 2)
        step(jnp.minimum(t + 2, 31), 0, t + 1, 1)
        pass_on(t + 1)
        return 0

    lax.fori_loop(0, 16, two, 0)
    for half in range(2):
        join(0, half, 1)

    token = lax.broadcasted_iota(jnp.int32, (1, ROWS), 1) // GROUP
    live = z * TOKENS + token < jnp.where(side == 0, len_ref[0], len_ref[1])
    done = jnp.where(live, acc[0, 0:WIDTH, :] / acc[0, WIDTH:WIDTH + 1, :], 0.0)
    turn[...] = done.T
    for j in range(GROUP):
        mixed[side, 0, :, j * WIDTH:(j + 1) * WIDTH] = turn[pl.ds(j, TOKENS, stride=GROUP), :].astype(BF16)

    def of_stream(stream):
        return side if stream == 0 else 1 - side

    def ag_copy(stream, n, slot):
        up = 1 if stream == 0 else 0
        to = jnp.where(slot % 2 == up, 1, -1)
        where = of_stream(stream)
        i = stream * RING + slot
        return remote(mixed.at[where, n], mixed.at[where, slot], ag_send.at[i], ag_recv.at[i], z_at(to))

    across = remote(mixed.at[side, 0], mixed.at[side, 0], mx_send, mx_recv, partner)
    across.start()
    for slot in (1, 2):
        ag_copy(0, 0, slot).start()

    def arrive(stream, n):
        ag_copy(stream, 0, n).wait_recv()

        @pl.when(n + 2 < RING)
        def _():
            ag_copy(stream, n, n + 2).start()

    def project(slot_own, slot_other, at):
        slot_0 = jnp.where(side == 0, slot_own, slot_other)
        slot_1 = jnp.where(side == 0, slot_other, slot_own)
        part[at, 0:TOKENS] = jnp.dot(mixed[0, slot_0], w_ref[...], preferred_element_type=F32)
        part[at, TOKENS:] = jnp.dot(mixed[1, slot_1], w_ref[...], preferred_element_type=F32)

        @pl.when((at // 2) % 2 != core)
        def _():
            to_mate(at).start()

    def to_mate(at):
        return remote(part.at[at], mate_in.at[at], co_send.at[at], co_recv.at[at], mate)

    def y_copy(index, to):
        return remote(y_out.at[index], y_in.at[y * 2 + index % 2], y_send.at[index], y_recv.at[y * 2 + index % 2], y_at(to))

    def spread(at):
        @pl.when((at // 2) % 2 == core)
        def _():
            to_mate(at).wait_recv()
            for half in range(2):
                to = half * 2 + at // 4
                index = to * 2 + at % 2
                rows = pl.ds(half * TOKENS, TOKENS)
                both = part[at, rows, :] + mate_in[at, rows, :]

                @pl.when(to == y)
                def _():
                    own[at % 2] = both

                @pl.when(to != y)
                def _():
                    y_out[index] = both.astype(BF16)
                    y_copy(index, to).start()

    across.wait_recv()
    for slot in (1, 2):
        ag_copy(1, 0, slot).start()
    project(0, 0, z)

    def below(d):
        return (z - d + RING) % RING

    def above(d):
        return (z + d) % RING

    def round_(d, _):
        for n in (2 * d - 1, 2 * d):
            for stream in range(2):
                arrive(stream, n)
        project(2 * d - 1, 2 * d, below(d))
        project(2 * d, 2 * d - 1, above(d))

        @pl.when(d == 1)
        def _():
            spread(z)

        @pl.when(d > 1)
        def _():
            spread(below(d - 1))
            spread(above(d - 1))

        return 0

    lax.fori_loop(1, 4, round_, 0)
    arrive(0, 7)
    arrive(1, 7)
    project(7, 7, above(4))
    spread(below(3))
    spread(above(3))
    spread(above(4))

    for which in range(2):
        total = own[which]
        for step_ in range(1, 4):
            source = (y + step_) % 4
            y_in_copy = remote(
                y_out.at[which], y_in.at[source * 2 + which], y_send.at[which], y_recv.at[source * 2 + which], y_at(source)
            )
            y_in_copy.wait_recv()
            total = total + y_in[source * 2 + which].astype(F32)
        out_ref[which * TOKENS:(which + 1) * TOKENS, :] = total

    for index in range(4):
        kv_copy(index).wait_send()

    def sent(slot, _):
        for half in range(2):
            q_copy(0, half, slot).wait_send()
            for copy in rs_copies(slot, half):
                copy.wait_send()
        for stream in range(2):
            ag_copy(stream, 0, slot).wait_send()
        return 0

    lax.fori_loop(1, RING, sent, 0)
    across.wait_send()

    def sent_at(at, _):
        @pl.when((at // 2) % 2 != core)
        def _():
            to_mate(at).wait_send()

        @pl.when(at // 2 != y)
        def _():
            y_copy(at, at // 2).wait_send()

        return 0

    lax.fori_loop(0, RING, sent_at, 0)


def body(queries, keys, values, lengths, prompt_lengths, out_weight):
    vmem = pl.BlockSpec(memory_space=pltpu.VMEM)
    smem = pl.BlockSpec(memory_space=pltpu.SMEM)
    dma = pltpu.SemaphoreType.DMA
    return pl.pallas_call(
        kernel,
        out_shape=jax.ShapeDtypeStruct((2 * TOKENS, COLUMNS), F32),
        in_specs=[vmem, vmem, vmem, smem, smem, vmem],
        out_specs=vmem,
        scratch_shapes=[
            pltpu.VMEM((RING, ROWS, WIDTH), BF16),
            pltpu.VMEM((4, SPAN, WIDTH), BF16),
            pltpu.VMEM((4, WIDTH + 16, SPAN), BF16),
            pltpu.VMEM((2, SPAN, ROWS), F32),
            pltpu.VMEM((2, 8, ROWS), F32),
            pltpu.VMEM((RING, WIDTH + 8, ROWS), F32),
            pltpu.VMEM((RING, 8, ROWS), F32),
            pltpu.VMEM((2 * RING, WIDTH, HALF), BF16),
            pltpu.VMEM((2 * RING, 16, HALF), F32),
            pltpu.VMEM((2 * RING, WIDTH, HALF), BF16),
            pltpu.VMEM((2 * RING, 16, HALF), F32),
            pltpu.VMEM((ROWS, WIDTH), F32),
            pltpu.VMEM((2, RING, TOKENS, FEATURES), BF16),
            pltpu.VMEM((RING, 2 * TOKENS, COLUMNS), F32),
            pltpu.VMEM((RING, 2 * TOKENS, COLUMNS), F32),
            pltpu.VMEM((8, TOKENS, COLUMNS), BF16),
            pltpu.VMEM((8, TOKENS, COLUMNS), BF16),
            pltpu.VMEM((2, TOKENS, COLUMNS), F32),
            dma((4,)), dma((4,)),
            dma((2 * RING,)), dma((2 * RING,)),
            dma((2 * RING,)), dma((2 * RING,)),
            dma((2 * RING,)), dma((2 * RING,)),
            dma, dma,
            dma((2 * RING,)), dma((2 * RING,)),
            dma((RING,)), dma((RING,)),
            dma((8,)), dma((8,)),
        ],
        compiler_params=pltpu.CompilerParams(
            collective_id=1, has_side_effects=True, vmem_limit_bytes=48 << 20
        ),
        name="paired_attention",
    )(
        queries.reshape(ROWS, WIDTH),
        keys.reshape(2 * SPAN, WIDTH),
        values.reshape(2 * SPAN, WIDTH),
        lengths,
        prompt_lengths,
        out_weight,
    )


def solution(mesh):
    in_specs = (
        P(("pair", "ctx"), "head", None),
        P(("pair", "ctx"), "head", None),
        P(("pair", "ctx"), "head", None),
        P("pair"),
        P("pair"),
        P("head", "ctx"),
    )
    out_specs = P(("pair", "head"), "ctx")
    return jax.shard_map(body, mesh=mesh, in_specs=in_specs, out_specs=out_specs, check_vma=False)
```

```python
import jax
import jax.numpy as jnp
from jax import lax
from jax.experimental import pallas as pl
from jax.experimental.pallas import tpu as pltpu
from jax.sharding import PartitionSpec as P

MESH = pl.DeviceIdType.MESH
F32 = jnp.float32
BF16 = jnp.bfloat16
NT = (((1,), (1,)), ((), ()))
NN = (((1,), (0,)), ((), ()))
HIDDEN = -(2.0 ** 100)
LOG2E = 1.4426950408889634

TOKENS = 64
GROUP = 8
WIDTH = 128
ROWS = TOKENS * GROUP
SPAN = 1024
STRIP = 256
RING = 8
FEATURES = GROUP * WIDTH
COLUMNS = 512
SCALE = WIDTH ** -0.5 * LOG2E
HALF = ROWS // 2
PIECES = 4
LANES = ROWS // PIECES
PART = TOKENS // PIECES
LATE = 10

VIA_X = (0, 1, 2, 5, 6)
VIA_Z = (3, 4, 7)


def rising(slot, piece):
    return slot % 2 == 1 if slot < 7 else piece % 2 == 0


def before(slot, piece):
    if slot == 7:
        return 5 if piece % 2 == 0 else 6
    return max(slot - 2, 0)


def long_way(piece):
    return (7, 5, 3, 1) if piece % 2 == 0 else (7, 6, 4, 2)


def short_way(piece):
    return (6, 4, 2) if piece % 2 == 0 else (5, 3, 1)


def kernel(
    q_ref, k_ref, v_ref, len_ref, plen_ref, w_ref, out_ref,
    k_in, v_in, w, q_all, k_all, vt_all, score, peak, acc, top,
    go, come, turn, mixed, part, mate_in, y_out, y_in, own,
    in_sem, kv_send, kv_recv, q_send, q_recv, rs_send, rs_recv,
    mx_send, ag_send, ag_recv, co_send, co_recv, y_send, y_recv,
):
    ctx = lax.axis_index("ctx")
    head = lax.axis_index("head")
    side, z = ctx // RING, ctx % RING
    y, core = head // 2, head % 2

    def z_at(step):
        return {"ctx": side * RING + (z + step + RING) % RING}

    def y_at(to):
        return {"head": to * 2 + core}

    partner = {"ctx": (1 - side) * RING + z}
    mate = {"head": y * 2 + 1 - core}

    def remote(src, dst, send, recv, to):
        return pltpu.make_async_remote_copy(
            src_ref=src, dst_ref=dst, send_sem=send, recv_sem=recv,
            device_id=to, device_id_type=MESH,
        )

    barrier = pltpu.get_barrier_semaphore()
    for to in (z_at(1), z_at(-1), partner, mate, y_at((y + 1) % 4), y_at((y + 2) % 4), y_at((y + 3) % 4)):
        pl.semaphore_signal(barrier, inc=1, device_id=to, device_id_type=MESH)

    q_load = pltpu.make_async_copy(q_ref, q_all.at[0], in_sem.at[0])
    k_load = pltpu.make_async_copy(k_ref, k_in, in_sem.at[1])
    v_load = pltpu.make_async_copy(v_ref, v_in, in_sem.at[2])
    w_load = pltpu.make_async_copy(w_ref, w, in_sem.at[3])
    for load in (k_load, v_load, q_load, w_load):
        load.start()

    plen = plen_ref[0]

    def chunk_start(chunk):
        holder = jnp.where(chunk < 2, side, 1 - side)
        return (holder * RING + z) * 2 * SPAN + (chunk % 2) * SPAN

    acc[...] = jnp.zeros_like(acc)
    top[...] = jnp.full_like(top, HIDDEN)
    for chunk in range(4):
        seen = chunk_start(chunk) + lax.broadcasted_iota(jnp.int32, (16, SPAN), 1) < plen
        vt_all[chunk, WIDTH:, :] = jnp.where(seen, 1.0, 0.0).astype(BF16)

    def seen_rows(chunk):
        return chunk_start(chunk) + lax.broadcasted_iota(jnp.int32, (SPAN, WIDTH), 0) < plen

    k_load.wait()
    for chunk in range(2):
        keys = k_in[pl.ds(chunk * SPAN, SPAN), :].astype(F32)
        k_all[chunk] = jnp.where(seen_rows(chunk), keys, keys[0:1, :]).astype(BF16)
    v_load.wait()
    for chunk in range(2):
        vals = jnp.where(seen_rows(chunk), v_in[pl.ds(chunk * SPAN, SPAN), :].astype(F32), 0.0)
        vt_all[chunk, 0:WIDTH, :] = vals.T.astype(BF16)
    q_load.wait()

    def q_copy(n, half, slot):
        to = jnp.where(slot % 2 == 1, 1, -1)
        rows = pl.ds(half * HALF, HALF)
        return remote(
            q_all.at[n, rows], q_all.at[slot, rows],
            q_send.at[slot * 2 + half], q_recv.at[slot * 2 + half], z_at(to),
        )

    def kv_copy(index):
        chunk = index // 2
        if index % 2 == 0:
            src, dst = k_all.at[chunk], k_all.at[chunk + 2]
        else:
            src, dst = vt_all.at[chunk, 0:WIDTH], vt_all.at[chunk + 2, 0:WIDTH]
        return remote(src, dst, kv_send.at[index], kv_recv.at[index], partner)

    pl.semaphore_wait(barrier, 7)
    kv_copy(0).start()
    for half in range(2):
        for slot in (1, 2):
            q_copy(0, half, slot).start()
    kv_copy(1).start()

    def task(t):
        n = jnp.where(t < 16, t // 2, jnp.where(t < 24, t - 16, 31 - t))
        chunk = jnp.where(t < 16, t % 2, jnp.where(t < 24, 2, 3))
        return n, chunk

    def ready(t):
        @pl.when(jnp.logical_and(jnp.logical_and(t >= 2, t < 16), t % 2 == 0))
        def _():
            n = t // 2
            for half in range(2):
                q_copy(0, half, n).wait_recv()

                @pl.when(n + 2 < RING)
                def _():
                    q_copy(n, half, n + 2).start()

        @pl.when(t == LATE)
        def _():
            kv_copy(2).start()
            kv_copy(3).start()

        @pl.when(t == 16)
        def _():
            kv_copy(0).wait_recv()

        @pl.when(t == 24)
        def _():
            kv_copy(2).wait_recv()

    def ready_values(t):
        @pl.when(t == 16)
        def _():
            kv_copy(1).wait_recv()

        @pl.when(t == 24)
        def _():
            kv_copy(3).wait_recv()

    def step(ahead, slot_ahead, now, slot_now):
        if ahead is not None:
            n_ahead, c_ahead = task(ahead)
            queries = q_all[n_ahead]
        if now is not None:
            n_now, c_now = task(now)
            best = peak[slot_now, 0:1, :]
        total = highest = None
        for strip in range(0, SPAN, STRIP):
            at = pl.ds(strip, STRIP)
            if ahead is not None:
                s = lax.dot_general(k_all[c_ahead, at, :], queries, NT, preferred_element_type=F32)
                score[slot_ahead, at, :] = s
                high = jnp.max(s.reshape(STRIP // 8, 8, ROWS), axis=0)
                highest = high if highest is None else jnp.maximum(highest, high)
            if now is not None:
                weights = jnp.exp2((score[slot_now, at, :] - best) * SCALE).astype(BF16)
                term = lax.dot_general(vt_all[c_now, :, at], weights, NN, preferred_element_type=F32)
                total = term if total is None else total + term
        if ahead is not None:
            peak[slot_ahead, 0:1, :] = jnp.max(highest, axis=0, keepdims=True).astype(BF16).astype(F32)
        if now is not None:
            best = jnp.where(chunk_start(c_now) < plen, best, HIDDEN)
            old = top[n_now, 0:1, :]
            new = jnp.maximum(old, best)
            top[n_now, 0:1, :] = new
            acc[n_now] = acc[n_now] * jnp.exp2((old - new) * SCALE) + total[0:136] * jnp.exp2((best - new) * SCALE)

    def rs_copy(slot, piece):
        i = slot * PIECES + piece
        to = -1 if rising(slot, piece) else 1
        return remote(go.at[i], come.at[i], rs_send.at[i], rs_recv.at[i], z_at(to))

    def pass_on(slot, piece):
        lanes = pl.ds(piece * LANES, LANES)
        i = slot * PIECES + piece
        go[i, 0:WIDTH, :] = acc[slot, 0:WIDTH, lanes].astype(BF16)
        total = acc[slot, WIDTH:WIDTH + 1, lanes]
        high = total.astype(BF16).astype(F32)
        row = lax.broadcasted_iota(jnp.int32, (16, LANES), 0)
        stats = jnp.where(row == 0, top[slot, 0:1, lanes], jnp.where(row == 1, high, jnp.where(row == 2, total - high, 0.0)))
        go[i, WIDTH:, :] = stats.astype(BF16)
        rs_copy(slot, piece).start()

    def join(slot, piece, source):
        rs_copy(source, piece).wait_recv()
        lanes = pl.ds(piece * LANES, LANES)
        i = source * PIECES + piece
        stats = come[i, WIDTH:, :].astype(F32)
        old, best = top[slot, 0:1, lanes], stats[0:1]
        new = jnp.maximum(old, best)
        keep, add = jnp.exp2((old - new) * SCALE), jnp.exp2((best - new) * SCALE)
        top[slot, 0:1, lanes] = new
        acc[slot, 0:WIDTH, lanes] = acc[slot, 0:WIDTH, lanes] * keep + come[i, 0:WIDTH, :].astype(F32) * add
        acc[slot, WIDTH:, lanes] = acc[slot, WIDTH:, lanes] * keep + (stats[1:2] + stats[2:3]) * add

    def first_sends(t):
        @pl.when(t == 24)
        def _():
            for piece in range(PIECES):
                pass_on(7, piece)

        @pl.when(t == 25)
        def _():
            for piece in range(0, PIECES, 2):
                pass_on(6, piece)

        @pl.when(t == 26)
        def _():
            for piece in range(1, PIECES, 2):
                pass_on(5, piece)

    ready(0)
    step(0, 0, None, None)

    def two(g, _):
        t = g * 2
        ready(t + 1)
        ready_values(t)
        step(t + 1, 1, t, 0)
        first_sends(t)
        ready(t + 2)
        step(jnp.minimum(t + 2, 31), 0, t + 1, 1)
        first_sends(t + 1)
        return 0

    lax.fori_loop(0, 16, two, 0)

    for level in range(1, 4):
        for piece in range(PIECES):
            way = long_way(piece)
            join(way[level], piece, way[level - 1])
            pass_on(way[level], piece)
        if level < 3:
            for piece in range(PIECES):
                way = short_way(piece ^ 1)
                join(way[level], piece ^ 1, way[level - 1])
                pass_on(way[level], piece ^ 1)

    def held(stream, slot, piece):
        return mixed.at[side if stream == 0 else 1 - side, slot, pl.ds(piece * PART, PART)]

    def ag_copy(stream, slot, piece):
        i = (stream * RING + slot) * PIECES + piece
        to = 1 if rising(slot, piece) else -1
        return remote(
            held(stream, before(slot, piece), piece), held(stream, slot, piece),
            ag_send.at[i], ag_recv.at[i], z_at(to),
        )

    def x_copy(slot, piece):
        i = slot * PIECES + piece
        return remote(
            held(0, slot, piece), held(0, slot, piece),
            mx_send.at[i], ag_recv.at[RING * PIECES + i], partner,
        )

    for piece in range(PIECES):
        join(0, piece, long_way(piece)[3])
        join(0, piece, short_way(piece)[2])
        lanes = pl.ds(piece * LANES, LANES)
        token = piece * PART + lax.broadcasted_iota(jnp.int32, (1, LANES), 1) // GROUP
        live = z * TOKENS + token < jnp.where(side == 0, len_ref[0], len_ref[1])
        done = jnp.where(live, acc[0, 0:WIDTH, lanes] / acc[0, WIDTH:WIDTH + 1, lanes], 0.0)
        turn[piece] = done.T
        for j in range(GROUP):
            mixed[side, 0, pl.ds(piece * PART, PART), j * WIDTH:(j + 1) * WIDTH] = turn[piece, pl.ds(j, PART, stride=GROUP), :].astype(BF16)
        ag_copy(0, 1, piece).start()
        ag_copy(0, 2, piece).start()
        x_copy(0, piece).start()

    def arrive(stream, slots):
        for piece in range(PIECES):
            for slot in slots:
                ag_copy(stream, slot, piece).wait_recv()
                for later in range(3, RING):
                    if before(later, piece) == slot and (stream == 0 or later in VIA_Z):
                        ag_copy(stream, later, piece).start()
                if stream == 0 and slot in VIA_X:
                    x_copy(slot, piece).start()

    def chip_of(slot):
        return (z + (-((slot + 1) // 2) if slot % 2 == 1 else slot // 2) + RING) % RING

    def to_mate(slot):
        return remote(part.at[slot], mate_in.at[slot], co_send.at[slot], co_recv.at[slot], mate)

    def given(slot):
        return (chip_of(slot) // 2) % 2 != core

    def project(slot):
        both = jnp.concatenate([mixed[0, slot], mixed[1, slot]], axis=0)
        part[slot] = jnp.dot(both, w[...], preferred_element_type=F32)

        @pl.when(given(slot))
        def _():
            to_mate(slot).start()

    def y_copy(index, to):
        return remote(y_out.at[index], y_in.at[y * 2 + index % 2], y_send.at[index], y_recv.at[y * 2 + index % 2], y_at(to))

    def spread(slot):
        at = chip_of(slot)

        @pl.when(jnp.logical_not(given(slot)))
        def _():
            to_mate(slot).wait_recv()
            for half in range(2):
                to = half * 2 + at // 4
                index = to * 2 + at % 2
                rows = pl.ds(half * TOKENS, TOKENS)
                both = part[slot, rows, :] + mate_in[slot, rows, :]

                @pl.when(to == y)
                def _():
                    own[at % 2] = both

                @pl.when(to != y)
                def _():
                    y_out[index] = both.astype(BF16)
                    y_copy(index, to).start()

    arrive(0, (1, 2))
    arrive(1, (0,))
    w_load.wait()
    project(0)
    arrive(0, (3, 4))
    arrive(1, (1, 2))
    project(1)
    project(2)
    spread(0)
    arrive(0, (5, 6))
    arrive(1, (3, 4))
    project(3)
    project(4)
    spread(1)
    spread(2)
    arrive(0, (7,))
    arrive(1, (5, 6))
    project(5)
    project(6)
    spread(3)
    spread(4)
    arrive(1, (7,))
    project(7)
    spread(5)
    spread(6)
    spread(7)

    for which in range(2):
        total = own[which]
        for further in range(1, 4):
            source = (y + further) % 4
            remote(
                y_out.at[which], y_in.at[source * 2 + which], y_send.at[which], y_recv.at[source * 2 + which], y_at(source)
            ).wait_recv()
            total = total + y_in[source * 2 + which].astype(F32)
        out_ref[which * TOKENS:(which + 1) * TOKENS, :] = total

    for index in range(4):
        kv_copy(index).wait_send()
    for slot in range(1, RING):
        for half in range(2):
            q_copy(0, half, slot).wait_send()
        for piece in range(PIECES):
            rs_copy(slot, piece).wait_send()
            ag_copy(0, slot, piece).wait_send()
    for piece in range(PIECES):
        for slot in VIA_Z:
            ag_copy(1, slot, piece).wait_send()
        for slot in VIA_X:
            x_copy(slot, piece).wait_send()
    for slot in range(RING):
        @pl.when(given(slot))
        def _():
            to_mate(slot).wait_send()

        @pl.when(slot // 2 != y)
        def _():
            y_copy(slot, slot // 2).wait_send()


def body(queries, keys, values, lengths, prompt_lengths, out_weight):
    hbm = pl.BlockSpec(memory_space=pltpu.HBM)
    smem = pl.BlockSpec(memory_space=pltpu.SMEM)
    dma = pltpu.SemaphoreType.DMA
    return pl.pallas_call(
        kernel,
        out_shape=jax.ShapeDtypeStruct((2 * TOKENS, COLUMNS), F32),
        in_specs=[hbm, hbm, hbm, smem, smem, hbm],
        out_specs=pl.BlockSpec(memory_space=pltpu.VMEM),
        scratch_shapes=[
            pltpu.VMEM((2 * SPAN, WIDTH), BF16),
            pltpu.VMEM((2 * SPAN, WIDTH), BF16),
            pltpu.VMEM((FEATURES, COLUMNS), BF16),
            pltpu.VMEM((RING, ROWS, WIDTH), BF16),
            pltpu.VMEM((4, SPAN, WIDTH), BF16),
            pltpu.VMEM((4, WIDTH + 16, SPAN), BF16),
            pltpu.VMEM((2, SPAN, ROWS), F32),
            pltpu.VMEM((2, 8, ROWS), F32),
            pltpu.VMEM((RING, WIDTH + 8, ROWS), F32),
            pltpu.VMEM((RING, 8, ROWS), F32),
            pltpu.VMEM((RING * PIECES, WIDTH + 16, LANES), BF16),
            pltpu.VMEM((RING * PIECES, WIDTH + 16, LANES), BF16),
            pltpu.VMEM((PIECES, LANES, WIDTH), F32),
            pltpu.VMEM((2, RING, TOKENS, FEATURES), BF16),
            pltpu.VMEM((RING, 2 * TOKENS, COLUMNS), F32),
            pltpu.VMEM((RING, 2 * TOKENS, COLUMNS), F32),
            pltpu.VMEM((8, TOKENS, COLUMNS), BF16),
            pltpu.VMEM((8, TOKENS, COLUMNS), BF16),
            pltpu.VMEM((2, TOKENS, COLUMNS), F32),
            dma((4,)),
            dma((4,)), dma((4,)),
            dma((2 * RING,)), dma((2 * RING,)),
            dma((RING * PIECES,)), dma((RING * PIECES,)),
            dma((RING * PIECES,)),
            dma((2 * RING * PIECES,)), dma((2 * RING * PIECES,)),
            dma((RING,)), dma((RING,)),
            dma((8,)), dma((8,)),
        ],
        compiler_params=pltpu.CompilerParams(
            collective_id=1, has_side_effects=True, vmem_limit_bytes=56 << 20
        ),
        name="paired_attention",
    )(
        queries.reshape(ROWS, WIDTH),
        keys.reshape(2 * SPAN, WIDTH),
        values.reshape(2 * SPAN, WIDTH),
        lengths,
        prompt_lengths,
        out_weight,
    )


def solution(mesh):
    in_specs = (
        P(("pair", "ctx"), "head", None),
        P(("pair", "ctx"), "head", None),
        P(("pair", "ctx"), "head", None),
        P("pair"),
        P("pair"),
        P("head", "ctx"),
    )
    out_specs = P(("pair", "head"), "ctx")
    return jax.shard_map(body, mesh=mesh, in_specs=in_specs, out_specs=out_specs, check_vma=False)
```

```python
import jax
import jax.numpy as jnp
from jax import lax
from jax.experimental import pallas as pl
from jax.experimental.pallas import tpu as pltpu
from jax.sharding import PartitionSpec as P

MESH = pl.DeviceIdType.MESH
F32 = jnp.float32
BF16 = jnp.bfloat16
NT = (((1,), (1,)), ((), ()))
NN = (((1,), (0,)), ((), ()))
HIDDEN = -(2.0 ** 100)
LOG2E = 1.4426950408889634

TOKENS = 64
GROUP = 8
WIDTH = 128
ROWS = TOKENS * GROUP
SPAN = 1024
STRIP = 256
RING = 8
FEATURES = GROUP * WIDTH
COLUMNS = 512
SCALE = WIDTH ** -0.5 * LOG2E
HALF = ROWS // 2
PIECES = 4
LANES = ROWS // PIECES
PART = TOKENS // PIECES
LATE = 10


def rising(slot, piece):
    return slot % 2 == 1 if slot < 7 else piece % 2 == 0


def before(slot, piece):
    if slot == 7:
        return 5 if piece % 2 == 0 else 6
    return max(slot - 2, 0)


def long_way(piece):
    return (7, 5, 3, 1) if piece % 2 == 0 else (7, 6, 4, 2)


def short_way(piece):
    return (6, 4, 2) if piece % 2 == 0 else (5, 3, 1)


def kernel(
    q_ref, k_ref, v_ref, len_ref, plen_ref, w_ref, out_ref,
    v_in, w_all, q_all, k_all, vt_all, score, peak, acc, top,
    go, come, turn, mixed, part, mate_in, y_out, y_in, own,
    in_sem, kv_send, kv_recv, q_send, q_recv, rs_send, rs_recv,
    w_send, w_recv, ag_send, ag_recv, co_send, co_recv, y_send, y_recv,
):
    ctx = lax.axis_index("ctx")
    head = lax.axis_index("head")
    side, z = ctx // RING, ctx % RING
    y, core = head // 2, head % 2

    def z_at(step):
        return {"ctx": side * RING + (z + step + RING) % RING}

    def y_at(to):
        return {"head": to * 2 + core}

    partner = {"ctx": (1 - side) * RING + z}
    mate = {"head": y * 2 + 1 - core}

    def opposite(to):
        return {"ctx": (1 - side) * RING + z, "head": to * 2 + core}

    def remote(src, dst, send, recv, to):
        return pltpu.make_async_remote_copy(
            src_ref=src, dst_ref=dst, send_sem=send, recv_sem=recv,
            device_id=to, device_id_type=MESH,
        )

    barrier = pltpu.get_barrier_semaphore()
    met = [z_at(1), z_at(-1), mate] + [y_at((y + step) % 4) for step in range(1, 4)] + [opposite(to) for to in range(4)]
    for to in met:
        pl.semaphore_signal(barrier, inc=1, device_id=to, device_id_type=MESH)

    loads = [
        pltpu.make_async_copy(k_ref.at[pl.ds(chunk * SPAN, SPAN)], k_all.at[chunk], in_sem.at[chunk]) for chunk in range(2)
    ]
    v_load = pltpu.make_async_copy(v_ref, v_in, in_sem.at[2])
    q_load = pltpu.make_async_copy(q_ref, q_all.at[0], in_sem.at[3])
    w_load = pltpu.make_async_copy(w_ref, w_all.at[side], in_sem.at[4])
    for load in (v_load, *loads, q_load, w_load):
        load.start()

    plen = plen_ref[0]

    def chunk_start(chunk):
        holder = jnp.where(chunk < 2, side, 1 - side)
        return (holder * RING + z) * 2 * SPAN + (chunk % 2) * SPAN

    def seen_rows(chunk):
        return chunk_start(chunk) + lax.broadcasted_iota(jnp.int32, (SPAN, WIDTH), 0) < plen

    def hide_keys(chunk):
        keys = k_all[chunk].astype(F32)
        k_all[chunk] = jnp.where(seen_rows(chunk), keys, keys[0:1, :]).astype(BF16)

    def turn_values(chunk):
        vals = jnp.where(seen_rows(chunk), v_in[pl.ds(chunk * SPAN, SPAN), :].astype(F32), 0.0)
        vt_all[chunk, 0:WIDTH, :] = vals.T.astype(BF16)

    def q_copy(n, half, slot):
        to = jnp.where(slot % 2 == 1, 1, -1)
        rows = pl.ds(half * HALF, HALF)
        src = q_ref.at[rows] if n is None else q_all.at[n, rows]
        return remote(src, q_all.at[slot, rows], q_send.at[slot * 2 + half], q_recv.at[slot * 2 + half], z_at(to))

    def kv_copy(index):
        chunk = index // 2
        if index % 2 == 0:
            src, dst = k_ref.at[pl.ds(chunk * SPAN, SPAN)], k_all.at[chunk + 2]
        else:
            src, dst = vt_all.at[chunk, 0:WIDTH], vt_all.at[chunk + 2, 0:WIDTH]
        return remote(src, dst, kv_send.at[index], kv_recv.at[index], partner)

    w_copy = remote(w_ref, w_all.at[side], w_send, w_recv, partner)

    acc[...] = jnp.zeros_like(acc)
    top[...] = jnp.full_like(top, HIDDEN)
    for chunk in range(4):
        seen = chunk_start(chunk) + lax.broadcasted_iota(jnp.int32, (16, SPAN), 1) < plen
        vt_all[chunk, WIDTH:, :] = jnp.where(seen, 1.0, 0.0).astype(BF16)

    pl.semaphore_wait(barrier, len(met))
    kv_copy(0).start()
    for half in range(2):
        for slot in (1, 2):
            q_copy(None, half, slot).start()
    v_load.wait()
    turn_values(0)
    kv_copy(1).start()
    turn_values(1)
    for chunk in range(2):
        loads[chunk].wait()
        hide_keys(chunk)
    q_load.wait()

    def task(t):
        n = jnp.where(t < 16, t // 2, jnp.where(t < 24, t - 16, 31 - t))
        chunk = jnp.where(t < 16, t % 2, jnp.where(t < 24, 2, 3))
        return n, chunk

    def ready(t):
        @pl.when(jnp.logical_and(jnp.logical_and(t >= 2, t < 16), t % 2 == 0))
        def _():
            n = t // 2
            for half in range(2):
                q_copy(None, half, n).wait_recv()

                @pl.when(n + 2 < RING)
                def _():
                    q_copy(n, half, n + 2).start()

        @pl.when(t == LATE)
        def _():
            kv_copy(2).start()
            kv_copy(3).start()

        @pl.when(t == 16)
        def _():
            kv_copy(0).wait_recv()
            hide_keys(2)

        @pl.when(t == 24)
        def _():
            kv_copy(2).wait_recv()
            hide_keys(3)

    def ready_values(t):
        @pl.when(t == 16)
        def _():
            kv_copy(1).wait_recv()

        @pl.when(t == 24)
        def _():
            kv_copy(3).wait_recv()
            w_copy.start()

    def step(ahead, slot_ahead, now, slot_now):
        if ahead is not None:
            n_ahead, c_ahead = task(ahead)
            queries = q_all[n_ahead]
        if now is not None:
            n_now, c_now = task(now)
            best = peak[slot_now, 0:1, :]
        total = highest = None
        for strip in range(0, SPAN, STRIP):
            at = pl.ds(strip, STRIP)
            if ahead is not None:
                s = lax.dot_general(k_all[c_ahead, at, :], queries, NT, preferred_element_type=F32)
                score[slot_ahead, at, :] = s
                high = jnp.max(s.reshape(STRIP // 8, 8, ROWS), axis=0)
                highest = high if highest is None else jnp.maximum(highest, high)
            if now is not None:
                weights = jnp.exp2((score[slot_now, at, :] - best) * SCALE).astype(BF16)
                term = lax.dot_general(vt_all[c_now, :, at], weights, NN, preferred_element_type=F32)
                total = term if total is None else total + term
        if ahead is not None:
            peak[slot_ahead, 0:1, :] = jnp.max(highest, axis=0, keepdims=True).astype(BF16).astype(F32)
        if now is not None:
            best = jnp.where(chunk_start(c_now) < plen, best, HIDDEN)
            old = top[n_now, 0:1, :]
            new = jnp.maximum(old, best)
            top[n_now, 0:1, :] = new
            acc[n_now] = acc[n_now] * jnp.exp2((old - new) * SCALE) + total[0:136] * jnp.exp2((best - new) * SCALE)

    def rs_copy(slot, piece):
        i = slot * PIECES + piece
        to = -1 if rising(slot, piece) else 1
        return remote(go.at[i], come.at[i], rs_send.at[i], rs_recv.at[i], z_at(to))

    def mine(slot, piece):
        lanes = pl.ds(piece * LANES, LANES)
        return acc[slot, 0:WIDTH, lanes], acc[slot, WIDTH:WIDTH + 1, lanes], top[slot, 0:1, lanes]

    def joined(state, piece, source):
        rs_copy(source, piece).wait_recv()
        sums, total, old = state
        i = source * PIECES + piece
        stats = come[i, WIDTH:, :].astype(F32)
        best = stats[0:1]
        new = jnp.maximum(old, best)
        keep, add = jnp.exp2((old - new) * SCALE), jnp.exp2((best - new) * SCALE)
        return sums * keep + come[i, 0:WIDTH, :].astype(F32) * add, total * keep + (stats[1:2] + stats[2:3]) * add, new

    def pass_on(slot, piece, state):
        sums, total, best = state
        i = slot * PIECES + piece
        go[i, 0:WIDTH, :] = sums.astype(BF16)
        high = total.astype(BF16).astype(F32)
        row = lax.broadcasted_iota(jnp.int32, (16, LANES), 0)
        stats = jnp.where(row == 0, best, jnp.where(row == 1, high, jnp.where(row == 2, total - high, 0.0)))
        go[i, WIDTH:, :] = stats.astype(BF16)
        rs_copy(slot, piece).start()

    def relay(way, level, piece):
        pass_on(way[level], piece, joined(mine(way[level], piece), piece, way[level - 1]))

    def relay_long(level):
        for piece in range(PIECES):
            relay(long_way(piece), level, piece)

    def relay_short(level):
        for piece in (1, 0, 3, 2):
            relay(short_way(piece), level, piece)

    def returns(t):
        @pl.when(t == 24)
        def _():
            for piece in range(PIECES):
                pass_on(7, piece, mine(7, piece))

        @pl.when(t == 25)
        def _():
            for piece in range(0, PIECES, 2):
                pass_on(6, piece, mine(6, piece))

        @pl.when(t == 26)
        def _():
            for piece in range(1, PIECES, 2):
                pass_on(5, piece, mine(5, piece))

        @pl.when(t == 28)
        def _():
            relay_long(1)

        @pl.when(t == 29)
        def _():
            relay_short(1)

    ready(0)
    step(0, 0, None, None)

    def two(g, _):
        t = g * 2
        ready(t + 1)
        ready_values(t)
        step(t + 1, 1, t, 0)
        returns(t)
        ready(t + 2)
        step(jnp.minimum(t + 2, 31), 0, t + 1, 1)
        returns(t + 1)
        return 0

    lax.fori_loop(0, 16, two, 0)

    relay_long(2)
    relay_short(2)
    relay_long(3)

    def ag_copy(slot, piece):
        i = slot * PIECES + piece
        rows = pl.ds(piece * PART, PART)
        to = 1 if rising(slot, piece) else -1
        return remote(mixed.at[before(slot, piece), rows], mixed.at[slot, rows], ag_send.at[i], ag_recv.at[i], z_at(to))

    def finish(piece):
        state = joined(mine(0, piece), piece, short_way(piece)[2])
        sums, total, _ = joined(state, piece, long_way(piece)[3])
        token = piece * PART + lax.broadcasted_iota(jnp.int32, (1, LANES), 1) // GROUP
        live = z * TOKENS + token < jnp.where(side == 0, len_ref[0], len_ref[1])
        done = jnp.where(live, sums / total, 0.0)
        turn[piece] = done.T
        for j in range(GROUP):
            mixed[0, pl.ds(piece * PART, PART), j * WIDTH:(j + 1) * WIDTH] = turn[piece, pl.ds(j, PART, stride=GROUP), :].astype(BF16)
        ag_copy(1, piece).start()
        ag_copy(2, piece).start()

    def arrive(*slots):
        for piece in range(PIECES):
            for slot in slots:
                ag_copy(slot, piece).wait_recv()
                for later in range(3, RING):
                    if before(later, piece) == slot:
                        ag_copy(later, piece).start()

    def chip_of(slot):
        return (z + (-((slot + 1) // 2) if slot % 2 == 1 else slot // 2) + RING) % RING

    def to_mate(slot, block):
        i = slot * 2 + block
        return remote(part.at[slot, block], mate_in.at[slot, block], co_send.at[i], co_recv.at[i], mate)

    def given(slot):
        return (chip_of(slot) // 2) % 2 != core

    def project(block, first, last):
        rows = mixed[first:last].reshape((last - first) * TOKENS, FEATURES)
        terms = jnp.dot(rows, w_all[block], preferred_element_type=F32)
        part[first:last, block] = terms.reshape(last - first, TOKENS, COLUMNS)

        for slot in range(first, last):
            @pl.when(given(slot))
            def _():
                to_mate(slot, block).start()

    def y_copy(block, far, which):
        i = (block * 2 + far) * 2 + which
        to = {"ctx": block * RING + z, "head": (2 * side + far) * 2 + core}
        return remote(y_out.at[i], y_in.at[y * 2 + which], y_send.at[i], y_recv.at[y * 2 + which], to)

    def stays(block, far):
        return jnp.logical_and(block == side, 2 * side + far == y)

    def spread(block, first, last):
        for slot in range(first, last):
            at = chip_of(slot)
            far, which = at // 4, at % 2

            @pl.when(jnp.logical_not(given(slot)))
            def _():
                to_mate(slot, block).wait_recv()
                both = part[slot, block] + mate_in[slot, block]

                @pl.when(stays(block, far))
                def _():
                    own[which] = both

                @pl.when(jnp.logical_not(stays(block, far)))
                def _():
                    y_out[(block * 2 + far) * 2 + which] = both.astype(BF16)
                    y_copy(block, far, which).start()

    there = 1 - side
    for piece in (1, 0, 2, 3):
        finish(piece)
    w_load.wait()
    arrive(1, 2)
    project(side, 0, 1)
    arrive(3, 4)
    project(side, 1, 3)
    spread(side, 0, 1)
    arrive(5, 6)
    project(side, 3, 5)
    spread(side, 1, 3)
    w_copy.wait_recv()
    project(there, 0, 5)
    project(side, 5, 7)
    spread(there, 0, 5)
    project(there, 5, 7)
    spread(side, 3, 7)
    spread(there, 5, 7)
    arrive(7)
    project(there, 7, 8)
    project(side, 7, 8)
    spread(there, 7, 8)
    spread(side, 7, 8)

    def taken(source, which):
        i = source * 2 + which
        remote(y_out.at[which], y_in.at[i], y_send.at[which], y_recv.at[i], opposite(source)).wait_recv()
        return y_in[i].astype(F32)

    for which in range(2):
        rows = pl.ds(which * TOKENS, TOKENS)

        @pl.when(y // 2 == side)
        def _():
            out_ref[rows, :] = own[which] + taken((y + 1) % 4, which) + taken((y + 2) % 4, which) + taken((y + 3) % 4, which)

        @pl.when(y // 2 != side)
        def _():
            out_ref[rows, :] = taken(0, which) + taken(1, which) + taken(2, which) + taken(3, which)

    for index in range(4):
        kv_copy(index).wait_send()
    for slot in range(1, RING):
        for half in range(2):
            q_copy(None, half, slot).wait_send()
        for piece in range(PIECES):
            rs_copy(slot, piece).wait_send()
            ag_copy(slot, piece).wait_send()
    w_copy.wait_send()
    for slot in range(RING):
        @pl.when(given(slot))
        def _():
            for block in range(2):
                to_mate(slot, block).wait_send()
    for block in range(2):
        for far in range(2):
            for which in range(2):
                @pl.when(jnp.logical_not(stays(block, far)))
                def _():
                    y_copy(block, far, which).wait_send()


def body(queries, keys, values, lengths, prompt_lengths, out_weight):
    hbm = pl.BlockSpec(memory_space=pltpu.HBM)
    smem = pl.BlockSpec(memory_space=pltpu.SMEM)
    dma = pltpu.SemaphoreType.DMA
    return pl.pallas_call(
        kernel,
        out_shape=jax.ShapeDtypeStruct((2 * TOKENS, COLUMNS), F32),
        in_specs=[hbm, hbm, hbm, smem, smem, hbm],
        out_specs=pl.BlockSpec(memory_space=pltpu.VMEM),
        scratch_shapes=[
            pltpu.VMEM((2 * SPAN, WIDTH), BF16),
            pltpu.VMEM((2, FEATURES, COLUMNS), BF16),
            pltpu.VMEM((RING, ROWS, WIDTH), BF16),
            pltpu.VMEM((4, SPAN, WIDTH), BF16),
            pltpu.VMEM((4, WIDTH + 16, SPAN), BF16),
            pltpu.VMEM((2, SPAN, ROWS), F32),
            pltpu.VMEM((2, 8, ROWS), F32),
            pltpu.VMEM((RING, WIDTH + 8, ROWS), F32),
            pltpu.VMEM((RING, 8, ROWS), F32),
            pltpu.VMEM((RING * PIECES, WIDTH + 16, LANES), BF16),
            pltpu.VMEM((RING * PIECES, WIDTH + 16, LANES), BF16),
            pltpu.VMEM((PIECES, LANES, WIDTH), F32),
            pltpu.VMEM((RING, TOKENS, FEATURES), BF16),
            pltpu.VMEM((RING, 2, TOKENS, COLUMNS), F32),
            pltpu.VMEM((RING, 2, TOKENS, COLUMNS), F32),
            pltpu.VMEM((8, TOKENS, COLUMNS), BF16),
            pltpu.VMEM((8, TOKENS, COLUMNS), BF16),
            pltpu.VMEM((2, TOKENS, COLUMNS), F32),
            dma((5,)),
            dma((4,)), dma((4,)),
            dma((2 * RING,)), dma((2 * RING,)),
            dma((RING * PIECES,)), dma((RING * PIECES,)),
            dma, dma,
            dma((RING * PIECES,)), dma((RING * PIECES,)),
            dma((2 * RING,)), dma((2 * RING,)),
            dma((8,)), dma((8,)),
        ],
        compiler_params=pltpu.CompilerParams(
            collective_id=1, has_side_effects=True, vmem_limit_bytes=56 << 20
        ),
        name="paired_attention",
    )(
        queries.reshape(ROWS, WIDTH),
        keys.reshape(2 * SPAN, WIDTH),
        values.reshape(2 * SPAN, WIDTH),
        lengths,
        prompt_lengths,
        out_weight,
    )


def solution(mesh):
    in_specs = (
        P(("pair", "ctx"), "head", None),
        P(("pair", "ctx"), "head", None),
        P(("pair", "ctx"), "head", None),
        P("pair"),
        P("pair"),
        P("head", "ctx"),
    )
    out_specs = P(("pair", "head"), "ctx")
    return jax.shard_map(body, mesh=mesh, in_specs=in_specs, out_specs=out_specs, check_vma=False)
```

```python
import jax
import jax.numpy as jnp
from jax import lax
from jax.experimental import pallas as pl
from jax.experimental.pallas import tpu as pltpu
from jax.sharding import PartitionSpec as P

MESH = pl.DeviceIdType.MESH
F32 = jnp.float32
BF16 = jnp.bfloat16
NT = (((1,), (1,)), ((), ()))
NN = (((1,), (0,)), ((), ()))
HIDDEN = -(2.0 ** 100)
LOG2E = 1.4426950408889634

TOKENS = 64
GROUP = 8
WIDTH = 128
ROWS = TOKENS * GROUP
SPAN = 1024
STRIP = 256
RING = 8
FEATURES = GROUP * WIDTH
COLUMNS = 512
SCALE = WIDTH ** -0.5 * LOG2E
HALF = ROWS // 2
PIECES = 4
LANES = ROWS // PIECES
PART = TOKENS // PIECES
LATE = 10


def rising(slot, piece):
    return slot % 2 == 1 if slot < 7 else piece % 2 == 0


def before(slot, piece):
    if slot == 7:
        return 5 if piece % 2 == 0 else 6
    return max(slot - 2, 0)


def long_way(piece):
    return (7, 5, 3, 1) if piece % 2 == 0 else (7, 6, 4, 2)


def short_way(piece):
    return (6, 4, 2) if piece % 2 == 0 else (5, 3, 1)


def kernel(
    q_ref, k_ref, v_ref, len_ref, plen_ref, w_ref, out_ref,
    v_in, w_all, q_all, k_all, vt_all, score, peak, acc, top,
    go, come, turn, mixed, part, mate_in, y_out, y_in, own,
    in_sem, kv_send, kv_recv, q_send, q_recv, rs_send, rs_recv,
    w_send, w_recv, ag_send, ag_recv, co_send, co_recv, y_send, y_recv,
):
    ctx = lax.axis_index("ctx")
    head = lax.axis_index("head")
    side, z = ctx // RING, ctx % RING
    y, core = head // 2, head % 2

    def z_at(step):
        return {"ctx": side * RING + (z + step + RING) % RING}

    def y_at(to):
        return {"head": to * 2 + core}

    partner = {"ctx": (1 - side) * RING + z}
    mate = {"head": y * 2 + 1 - core}

    def opposite(to):
        return {"ctx": (1 - side) * RING + z, "head": to * 2 + core}

    def remote(src, dst, send, recv, to):
        return pltpu.make_async_remote_copy(
            src_ref=src, dst_ref=dst, send_sem=send, recv_sem=recv,
            device_id=to, device_id_type=MESH,
        )

    barrier = pltpu.get_barrier_semaphore()
    met = [z_at(1), z_at(-1), mate] + [y_at((y + step) % 4) for step in range(1, 4)] + [opposite(to) for to in range(4)]
    for to in met:
        pl.semaphore_signal(barrier, inc=1, device_id=to, device_id_type=MESH)

    loads = [
        pltpu.make_async_copy(k_ref.at[pl.ds(chunk * SPAN, SPAN)], k_all.at[chunk], in_sem.at[chunk]) for chunk in range(2)
    ]
    v_load = pltpu.make_async_copy(v_ref, v_in, in_sem.at[2])
    q_load = pltpu.make_async_copy(q_ref, q_all.at[0], in_sem.at[3])
    w_load = pltpu.make_async_copy(w_ref, w_all.at[side], in_sem.at[4])
    for load in (v_load, *loads, q_load, w_load):
        load.start()

    plen = plen_ref[0]

    def chunk_start(chunk):
        holder = jnp.where(chunk < 2, side, 1 - side)
        return (holder * RING + z) * 2 * SPAN + (chunk % 2) * SPAN

    def seen_rows(chunk):
        return chunk_start(chunk) + lax.broadcasted_iota(jnp.int32, (SPAN, WIDTH), 0) < plen

    def hide_keys(chunk):
        keys = k_all[chunk].astype(F32)
        k_all[chunk] = jnp.where(seen_rows(chunk), keys, keys[0:1, :]).astype(BF16)

    def turn_values(chunk):
        vals = jnp.where(seen_rows(chunk), v_in[pl.ds(chunk * SPAN, SPAN), :].astype(F32), 0.0)
        vt_all[chunk, 0:WIDTH, :] = vals.T.astype(BF16)

    def q_copy(n, half, slot):
        to = jnp.where(slot % 2 == 1, 1, -1)
        rows = pl.ds(half * HALF, HALF)
        src = q_ref.at[rows] if n is None else q_all.at[n, rows]
        return remote(src, q_all.at[slot, rows], q_send.at[slot * 2 + half], q_recv.at[slot * 2 + half], z_at(to))

    def kv_copy(index):
        chunk = index // 2
        if index % 2 == 0:
            src, dst = k_ref.at[pl.ds(chunk * SPAN, SPAN)], k_all.at[chunk + 2]
        else:
            src, dst = vt_all.at[chunk, 0:WIDTH], vt_all.at[chunk + 2, 0:WIDTH]
        return remote(src, dst, kv_send.at[index], kv_recv.at[index], partner)

    w_copy = remote(w_ref, w_all.at[side], w_send, w_recv, partner)

    acc[...] = jnp.zeros_like(acc)
    top[...] = jnp.full_like(top, HIDDEN)
    for chunk in range(4):
        seen = chunk_start(chunk) + lax.broadcasted_iota(jnp.int32, (16, SPAN), 1) < plen
        vt_all[chunk, WIDTH:, :] = jnp.where(seen, 1.0, 0.0).astype(BF16)

    pl.semaphore_wait(barrier, len(met))
    kv_copy(0).start()
    for half in range(2):
        for slot in (1, 2):
            q_copy(None, half, slot).start()
    v_load.wait()
    turn_values(0)
    kv_copy(1).start()
    turn_values(1)
    for chunk in range(2):
        loads[chunk].wait()
        hide_keys(chunk)
    q_load.wait()

    def task(t):
        n = jnp.where(t < 16, t // 2, jnp.where(t < 24, t - 16, 31 - t))
        chunk = jnp.where(t < 16, t % 2, jnp.where(t < 24, 2, 3))
        return n, chunk

    def ready(t):
        @pl.when(jnp.logical_and(jnp.logical_and(t >= 2, t < 16), t % 2 == 0))
        def _():
            n = t // 2
            for half in range(2):
                q_copy(None, half, n).wait_recv()

                @pl.when(n + 2 < RING)
                def _():
                    q_copy(n, half, n + 2).start()

        @pl.when(t == LATE)
        def _():
            kv_copy(2).start()
            kv_copy(3).start()

        @pl.when(t == 16)
        def _():
            kv_copy(0).wait_recv()
            hide_keys(2)

        @pl.when(t == 24)
        def _():
            kv_copy(2).wait_recv()
            hide_keys(3)

    def ready_values(t):
        @pl.when(t == 16)
        def _():
            kv_copy(1).wait_recv()

        @pl.when(t == 24)
        def _():
            kv_copy(3).wait_recv()
            w_copy.start()

    def step(ahead, slot_ahead, now, slot_now):
        if ahead is not None:
            n_ahead, c_ahead = task(ahead)
            queries = q_all[n_ahead]
        if now is not None:
            n_now, c_now = task(now)
            best = peak[slot_now, 0:1, :]
        total = highest = None
        for strip in range(0, SPAN, STRIP):
            at = pl.ds(strip, STRIP)
            if ahead is not None:
                s = lax.dot_general(k_all[c_ahead, at, :], queries, NT, preferred_element_type=F32)
                score[slot_ahead, at, :] = s
                high = jnp.max(s.reshape(STRIP // 8, 8, ROWS), axis=0)
                highest = high if highest is None else jnp.maximum(highest, high)
            if now is not None:
                weights = jnp.exp2((score[slot_now, at, :] - best) * SCALE).astype(BF16)
                term = lax.dot_general(vt_all[c_now, :, at], weights, NN, preferred_element_type=F32)
                total = term if total is None else total + term
        if ahead is not None:
            peak[slot_ahead, 0:1, :] = jnp.max(highest, axis=0, keepdims=True).astype(BF16).astype(F32)
        if now is not None:
            best = jnp.where(chunk_start(c_now) < plen, best, HIDDEN)
            old = top[n_now, 0:1, :]
            new = jnp.maximum(old, best)
            top[n_now, 0:1, :] = new
            acc[n_now] = acc[n_now] * jnp.exp2((old - new) * SCALE) + total[0:136] * jnp.exp2((best - new) * SCALE)

    def rs_copy(slot, piece):
        i = slot * PIECES + piece
        to = -1 if rising(slot, piece) else 1
        return remote(go.at[i], come.at[i], rs_send.at[i], rs_recv.at[i], z_at(to))

    def mine(slot, piece):
        lanes = pl.ds(piece * LANES, LANES)
        return acc[slot, 0:WIDTH, lanes], acc[slot, WIDTH:WIDTH + 1, lanes], top[slot, 0:1, lanes]

    def joined(state, piece, source):
        rs_copy(source, piece).wait_recv()
        sums, total, old = state
        i = source * PIECES + piece
        stats = come[i, WIDTH:, :].astype(F32)
        best = stats[0:1]
        new = jnp.maximum(old, best)
        keep, add = jnp.exp2((old - new) * SCALE), jnp.exp2((best - new) * SCALE)
        return sums * keep + come[i, 0:WIDTH, :].astype(F32) * add, total * keep + (stats[1:2] + stats[2:3]) * add, new

    def pass_on(slot, piece, state):
        sums, total, best = state
        i = slot * PIECES + piece
        go[i, 0:WIDTH, :] = sums.astype(BF16)
        high = total.astype(BF16).astype(F32)
        row = lax.broadcasted_iota(jnp.int32, (16, LANES), 0)
        stats = jnp.where(row == 0, best, jnp.where(row == 1, high, jnp.where(row == 2, total - high, 0.0)))
        go[i, WIDTH:, :] = stats.astype(BF16)
        rs_copy(slot, piece).start()

    def relay(way, level, piece):
        pass_on(way[level], piece, joined(mine(way[level], piece), piece, way[level - 1]))

    def relay_long(level):
        for piece in range(PIECES):
            relay(long_way(piece), level, piece)

    def relay_short(level):
        for piece in (1, 0, 3, 2):
            relay(short_way(piece), level, piece)

    def returns(t):
        @pl.when(t == 24)
        def _():
            for piece in range(PIECES):
                pass_on(7, piece, mine(7, piece))

        @pl.when(t == 25)
        def _():
            for piece in range(0, PIECES, 2):
                pass_on(6, piece, mine(6, piece))

        @pl.when(t == 26)
        def _():
            for piece in range(1, PIECES, 2):
                pass_on(5, piece, mine(5, piece))

        @pl.when(t == 28)
        def _():
            relay_long(1)

        @pl.when(t == 29)
        def _():
            relay_short(1)

    ready(0)
    step(0, 0, None, None)

    def two(g, _):
        t = g * 2
        ready(t + 1)
        ready_values(t)
        step(t + 1, 1, t, 0)
        returns(t)
        ready(t + 2)
        step(jnp.minimum(t + 2, 31), 0, t + 1, 1)
        returns(t + 1)
        return 0

    lax.fori_loop(0, 16, two, 0)

    relay_long(2)
    relay_short(2)
    relay_long(3)

    def ag_copy(slot, piece):
        i = slot * PIECES + piece
        rows = pl.ds(piece * PART, PART)
        to = 1 if rising(slot, piece) else -1
        return remote(mixed.at[before(slot, piece), rows], mixed.at[slot, rows], ag_send.at[i], ag_recv.at[i], z_at(to))

    def finish(piece):
        state = joined(mine(0, piece), piece, short_way(piece)[2])
        sums, total, _ = joined(state, piece, long_way(piece)[3])
        token = piece * PART + lax.broadcasted_iota(jnp.int32, (1, LANES), 1) // GROUP
        live = z * TOKENS + token < jnp.where(side == 0, len_ref[0], len_ref[1])
        done = jnp.where(live, sums / total, 0.0)
        turn[piece] = done.T
        for j in range(GROUP):
            mixed[0, pl.ds(piece * PART, PART), j * WIDTH:(j + 1) * WIDTH] = turn[piece, pl.ds(j, PART, stride=GROUP), :].astype(BF16)
        ag_copy(1, piece).start()
        ag_copy(2, piece).start()

    def arrive(*slots):
        for piece in range(PIECES):
            for slot in slots:
                ag_copy(slot, piece).wait_recv()
                for later in range(3, RING):
                    if before(later, piece) == slot:
                        ag_copy(later, piece).start()

    def chip_of(slot):
        return (z + (-((slot + 1) // 2) if slot % 2 == 1 else slot // 2) + RING) % RING

    def to_mate(slot, block):
        i = slot * 2 + block
        return remote(part.at[slot, block], mate_in.at[slot, block], co_send.at[i], co_recv.at[i], mate)

    def given(slot):
        return (chip_of(slot) // 2) % 2 != core

    def project(block, first, last):
        rows = mixed[first:last].reshape((last - first) * TOKENS, FEATURES)
        terms = jnp.dot(rows, w_all[block], preferred_element_type=F32)
        part[first:last, block] = terms.reshape(last - first, TOKENS, COLUMNS)

        for slot in range(first, last):
            @pl.when(given(slot))
            def _():
                to_mate(slot, block).start()

    def y_copy(block, far, which):
        i = (block * 2 + far) * 2 + which
        to = {"ctx": block * RING + z, "head": (2 * side + far) * 2 + core}
        return remote(y_out.at[i], y_in.at[y * 2 + which], y_send.at[i], y_recv.at[y * 2 + which], to)

    def stays(block, far):
        return jnp.logical_and(block == side, 2 * side + far == y)

    def spread(block, first, last):
        for slot in range(first, last):
            at = chip_of(slot)
            far, which = at // 4, at % 2

            @pl.when(jnp.logical_not(given(slot)))
            def _():
                to_mate(slot, block).wait_recv()
                both = part[slot, block] + mate_in[slot, block]

                @pl.when(stays(block, far))
                def _():
                    own[which] = both

                @pl.when(jnp.logical_not(stays(block, far)))
                def _():
                    y_out[(block * 2 + far) * 2 + which] = both.astype(BF16)
                    y_copy(block, far, which).start()

    there = 1 - side
    for piece in range(PIECES):
        finish(piece)
    w_load.wait()
    arrive(1, 2)
    arrive(3, 4)
    project(side, 0, 3)
    arrive(5, 6)
    project(side, 3, 5)
    spread(side, 0, 3)
    w_copy.wait_recv()
    project(there, 0, 5)
    project(side, 5, 7)
    spread(there, 0, 5)
    project(there, 5, 7)
    spread(side, 3, 7)
    spread(there, 5, 7)
    arrive(7)
    project(there, 7, 8)
    project(side, 7, 8)
    spread(there, 7, 8)
    spread(side, 7, 8)

    def taken(source, which):
        i = source * 2 + which
        remote(y_out.at[which], y_in.at[i], y_send.at[which], y_recv.at[i], opposite(source)).wait_recv()
        return y_in[i].astype(F32)

    for which in range(2):
        rows = pl.ds(which * TOKENS, TOKENS)

        @pl.when(y // 2 == side)
        def _():
            out_ref[rows, :] = own[which] + taken((y + 1) % 4, which) + taken((y + 2) % 4, which) + taken((y + 3) % 4, which)

        @pl.when(y // 2 != side)
        def _():
            out_ref[rows, :] = taken(0, which) + taken(1, which) + taken(2, which) + taken(3, which)

    for index in range(4):
        kv_copy(index).wait_send()
    for slot in range(1, RING):
        for half in range(2):
            q_copy(None, half, slot).wait_send()
        for piece in range(PIECES):
            rs_copy(slot, piece).wait_send()
            ag_copy(slot, piece).wait_send()
    w_copy.wait_send()
    for slot in range(RING):
        @pl.when(given(slot))
        def _():
            for block in range(2):
                to_mate(slot, block).wait_send()
    for block in range(2):
        for far in range(2):
            for which in range(2):
                @pl.when(jnp.logical_not(stays(block, far)))
                def _():
                    y_copy(block, far, which).wait_send()


def body(queries, keys, values, lengths, prompt_lengths, out_weight):
    hbm = pl.BlockSpec(memory_space=pltpu.HBM)
    smem = pl.BlockSpec(memory_space=pltpu.SMEM)
    dma = pltpu.SemaphoreType.DMA
    return pl.pallas_call(
        kernel,
        out_shape=pltpu.VMEM((2 * TOKENS, COLUMNS), F32),
        in_specs=[hbm, hbm, hbm, smem, smem, hbm],
        out_specs=pl.BlockSpec(memory_space=pltpu.VMEM),
        scratch_shapes=[
            pltpu.VMEM((2 * SPAN, WIDTH), BF16),
            pltpu.VMEM((2, FEATURES, COLUMNS), BF16),
            pltpu.VMEM((RING, ROWS, WIDTH), BF16),
            pltpu.VMEM((4, SPAN, WIDTH), BF16),
            pltpu.VMEM((4, WIDTH + 16, SPAN), BF16),
            pltpu.VMEM((2, SPAN, ROWS), F32),
            pltpu.VMEM((2, 8, ROWS), F32),
            pltpu.VMEM((RING, WIDTH + 8, ROWS), F32),
            pltpu.VMEM((RING, 8, ROWS), F32),
            pltpu.VMEM((RING * PIECES, WIDTH + 16, LANES), BF16),
            pltpu.VMEM((RING * PIECES, WIDTH + 16, LANES), BF16),
            pltpu.VMEM((PIECES, LANES, WIDTH), F32),
            pltpu.VMEM((RING, TOKENS, FEATURES), BF16),
            pltpu.VMEM((RING, 2, TOKENS, COLUMNS), F32),
            pltpu.VMEM((RING, 2, TOKENS, COLUMNS), F32),
            pltpu.VMEM((8, TOKENS, COLUMNS), BF16),
            pltpu.VMEM((8, TOKENS, COLUMNS), BF16),
            pltpu.VMEM((2, TOKENS, COLUMNS), F32),
            dma((5,)),
            dma((4,)), dma((4,)),
            dma((2 * RING,)), dma((2 * RING,)),
            dma((RING * PIECES,)), dma((RING * PIECES,)),
            dma, dma,
            dma((RING * PIECES,)), dma((RING * PIECES,)),
            dma((2 * RING,)), dma((2 * RING,)),
            dma((8,)), dma((8,)),
        ],
        compiler_params=pltpu.CompilerParams(
            collective_id=1, has_side_effects=True, vmem_limit_bytes=56 << 20
        ),
        name="paired_attention",
    )(
        queries.reshape(ROWS, WIDTH),
        keys.reshape(2 * SPAN, WIDTH),
        values.reshape(2 * SPAN, WIDTH),
        lengths,
        prompt_lengths,
        out_weight,
    )


def solution(mesh):
    in_specs = (
        P(("pair", "ctx"), "head", None),
        P(("pair", "ctx"), "head", None),
        P(("pair", "ctx"), "head", None),
        P("pair"),
        P("pair"),
        P("head", "ctx"),
    )
    out_specs = P(("pair", "head"), "ctx")
    return jax.shard_map(body, mesh=mesh, in_specs=in_specs, out_specs=out_specs, check_vma=False)
```

```python
import jax
import jax.numpy as jnp
from jax import lax
from jax.experimental import pallas as pl
from jax.experimental.pallas import tpu as pltpu
from jax.sharding import PartitionSpec as P

MESH = pl.DeviceIdType.MESH
F32 = jnp.float32
BF16 = jnp.bfloat16
NT = (((1,), (1,)), ((), ()))
NN = (((1,), (0,)), ((), ()))
HIDDEN = -(2.0 ** 100)
LOG2E = 1.4426950408889634

TOKENS = 64
GROUP = 8
WIDTH = 128
ROWS = TOKENS * GROUP
SPAN = 1024
STRIP = 256
RING = 8
FEATURES = GROUP * WIDTH
COLUMNS = 512
SCALE = WIDTH ** -0.5 * LOG2E
HALF = ROWS // 2
PIECES = 4
LANES = ROWS // PIECES
PART = TOKENS // PIECES
LATE = 10


def rising(slot, piece):
    return slot % 2 == 1 if slot < 7 else piece % 2 == 0


def before(slot, piece):
    if slot == 7:
        return 5 if piece % 2 == 0 else 6
    return max(slot - 2, 0)


def long_way(piece):
    return (7, 5, 3, 1) if piece % 2 == 0 else (7, 6, 4, 2)


def short_way(piece):
    return (6, 4, 2) if piece % 2 == 0 else (5, 3, 1)


def kernel(
    q_ref, k_ref, v_ref, len_ref, plen_ref, w_ref, out_ref,
    v_in, w_all, q_all, k_all, vt_all, score, peak, acc, top,
    go, come, turn, mixed, part, mate_in, y_out, y_in, own,
    in_sem, kv_send, kv_recv, q_send, q_recv, rs_send, rs_recv,
    w_send, w_recv, ag_send, ag_recv, co_send, co_recv, y_send, y_recv,
):
    ctx = lax.axis_index("ctx")
    head = lax.axis_index("head")
    side, z = ctx // RING, ctx % RING
    y, core = head // 2, head % 2

    def z_at(step):
        return {"ctx": side * RING + (z + step + RING) % RING}

    def y_at(to):
        return {"head": to * 2 + core}

    partner = {"ctx": (1 - side) * RING + z}
    mate = {"head": y * 2 + 1 - core}

    def opposite(to):
        return {"ctx": (1 - side) * RING + z, "head": to * 2 + core}

    def remote(src, dst, send, recv, to):
        return pltpu.make_async_remote_copy(
            src_ref=src, dst_ref=dst, send_sem=send, recv_sem=recv,
            device_id=to, device_id_type=MESH,
        )

    barrier = pltpu.get_barrier_semaphore()
    met = [z_at(1), z_at(-1), mate] + [y_at((y + step) % 4) for step in range(1, 4)] + [opposite(to) for to in range(4)]
    for to in met:
        pl.semaphore_signal(barrier, inc=1, device_id=to, device_id_type=MESH)

    loads = [
        pltpu.make_async_copy(k_ref.at[pl.ds(chunk * SPAN, SPAN)], k_all.at[chunk], in_sem.at[chunk]) for chunk in range(2)
    ]
    v_load = pltpu.make_async_copy(v_ref, v_in, in_sem.at[2])
    q_load = pltpu.make_async_copy(q_ref, q_all.at[0], in_sem.at[3])
    w_load = pltpu.make_async_copy(w_ref, w_all.at[side], in_sem.at[4])
    for load in (v_load, *loads, q_load, w_load):
        load.start()

    plen = plen_ref[0]

    def chunk_start(chunk):
        holder = jnp.where(chunk < 2, side, 1 - side)
        return (holder * RING + z) * 2 * SPAN + (chunk % 2) * SPAN

    def seen_rows(chunk):
        return chunk_start(chunk) + lax.broadcasted_iota(jnp.int32, (SPAN, WIDTH), 0) < plen

    def hide_keys(chunk):
        keys = k_all[chunk].astype(F32)
        k_all[chunk] = jnp.where(seen_rows(chunk), keys, keys[0:1, :]).astype(BF16)

    def turn_values(chunk):
        vals = jnp.where(seen_rows(chunk), v_in[pl.ds(chunk * SPAN, SPAN), :].astype(F32), 0.0)
        vt_all[chunk, 0:WIDTH, :] = vals.T.astype(BF16)

    def q_copy(n, half, slot):
        to = jnp.where(slot % 2 == 1, 1, -1)
        rows = pl.ds(half * HALF, HALF)
        src = q_ref.at[rows] if n is None else q_all.at[n, rows]
        return remote(src, q_all.at[slot, rows], q_send.at[slot * 2 + half], q_recv.at[slot * 2 + half], z_at(to))

    def kv_copy(index):
        chunk = index // 2
        if index % 2 == 0:
            src, dst = k_ref.at[pl.ds(chunk * SPAN, SPAN)], k_all.at[chunk + 2]
        else:
            src, dst = vt_all.at[chunk, 0:WIDTH], vt_all.at[chunk + 2, 0:WIDTH]
        return remote(src, dst, kv_send.at[index], kv_recv.at[index], partner)

    w_copy = remote(w_ref, w_all.at[side], w_send, w_recv, partner)

    acc[...] = jnp.zeros_like(acc)
    top[...] = jnp.full_like(top, HIDDEN)
    for chunk in range(4):
        seen = chunk_start(chunk) + lax.broadcasted_iota(jnp.int32, (16, SPAN), 1) < plen
        vt_all[chunk, WIDTH:, :] = jnp.where(seen, 1.0, 0.0).astype(BF16)

    pl.semaphore_wait(barrier, len(met))
    kv_copy(0).start()
    for half in range(2):
        for slot in (1, 2):
            q_copy(None, half, slot).start()
    v_load.wait()
    turn_values(0)
    kv_copy(1).start()
    turn_values(1)
    for chunk in range(2):
        loads[chunk].wait()
        hide_keys(chunk)
    q_load.wait()

    def task(t):
        n = jnp.where(t < 16, t // 2, jnp.where(t < 24, t - 16, 31 - t))
        chunk = jnp.where(t < 16, t % 2, jnp.where(t < 24, 2, 3))
        return n, chunk

    def ready(t):
        @pl.when(jnp.logical_and(jnp.logical_and(t >= 2, t < 16), t % 2 == 0))
        def _():
            n = t // 2
            for half in range(2):
                q_copy(None, half, n).wait_recv()

                @pl.when(n + 2 < RING)
                def _():
                    q_copy(n, half, n + 2).start()

        @pl.when(t == LATE)
        def _():
            kv_copy(2).start()
            kv_copy(3).start()

        @pl.when(t == 16)
        def _():
            kv_copy(0).wait_recv()
            hide_keys(2)

        @pl.when(t == 24)
        def _():
            kv_copy(2).wait_recv()
            hide_keys(3)

    def ready_values(t):
        @pl.when(t == 16)
        def _():
            kv_copy(1).wait_recv()

        @pl.when(t == 24)
        def _():
            kv_copy(3).wait_recv()
            w_copy.start()

    def step(ahead, slot_ahead, now, slot_now):
        if ahead is not None:
            n_ahead, c_ahead = task(ahead)
            queries = q_all[n_ahead]
        if now is not None:
            n_now, c_now = task(now)
            best = peak[slot_now, 0:1, :]
        total = highest = None
        for strip in range(0, SPAN, STRIP):
            at = pl.ds(strip, STRIP)
            if ahead is not None:
                s = lax.dot_general(k_all[c_ahead, at, :], queries, NT, preferred_element_type=F32)
                score[slot_ahead, at, :] = s
                high = jnp.max(s.reshape(STRIP // 8, 8, ROWS), axis=0)
                highest = high if highest is None else jnp.maximum(highest, high)
            if now is not None:
                weights = jnp.exp2((score[slot_now, at, :] - best) * SCALE).astype(BF16)
                term = lax.dot_general(vt_all[c_now, :, at], weights, NN, preferred_element_type=F32)
                total = term if total is None else total + term
        if ahead is not None:
            peak[slot_ahead, 0:1, :] = jnp.max(highest, axis=0, keepdims=True).astype(BF16).astype(F32)
        if now is not None:
            best = jnp.where(chunk_start(c_now) < plen, best, HIDDEN)
            old = top[n_now, 0:1, :]
            new = jnp.maximum(old, best)
            top[n_now, 0:1, :] = new
            acc[n_now] = acc[n_now] * jnp.exp2((old - new) * SCALE) + total[0:136] * jnp.exp2((best - new) * SCALE)

    def rs_copy(slot, piece):
        i = slot * PIECES + piece
        to = -1 if rising(slot, piece) else 1
        return remote(go.at[i], come.at[i], rs_send.at[i], rs_recv.at[i], z_at(to))

    def mine(slot, piece):
        lanes = pl.ds(piece * LANES, LANES)
        return acc[slot, 0:WIDTH, lanes], acc[slot, WIDTH:WIDTH + 1, lanes], top[slot, 0:1, lanes]

    def joined(state, piece, source):
        rs_copy(source, piece).wait_recv()
        sums, total, old = state
        i = source * PIECES + piece
        stats = come[i, WIDTH:, :].astype(F32)
        best = stats[0:1]
        new = jnp.maximum(old, best)
        keep, add = jnp.exp2((old - new) * SCALE), jnp.exp2((best - new) * SCALE)
        return sums * keep + come[i, 0:WIDTH, :].astype(F32) * add, total * keep + (stats[1:2] + stats[2:3]) * add, new

    def pass_on(slot, piece, state):
        sums, total, best = state
        i = slot * PIECES + piece
        go[i, 0:WIDTH, :] = sums.astype(BF16)
        high = total.astype(BF16).astype(F32)
        row = lax.broadcasted_iota(jnp.int32, (16, LANES), 0)
        stats = jnp.where(row == 0, best, jnp.where(row == 1, high, jnp.where(row == 2, total - high, 0.0)))
        go[i, WIDTH:, :] = stats.astype(BF16)
        rs_copy(slot, piece).start()

    def relay(way, level, piece):
        pass_on(way[level], piece, joined(mine(way[level], piece), piece, way[level - 1]))

    def relay_long(level):
        for piece in range(PIECES):
            relay(long_way(piece), level, piece)

    def relay_short(level):
        for piece in (1, 0, 3, 2):
            relay(short_way(piece), level, piece)

    def returns(t):
        @pl.when(t == 24)
        def _():
            for piece in range(PIECES):
                pass_on(7, piece, mine(7, piece))

        @pl.when(t == 25)
        def _():
            for piece in range(0, PIECES, 2):
                pass_on(6, piece, mine(6, piece))

        @pl.when(t == 26)
        def _():
            for piece in range(1, PIECES, 2):
                pass_on(5, piece, mine(5, piece))

        @pl.when(t == 28)
        def _():
            relay_long(1)

        @pl.when(t == 29)
        def _():
            relay_short(1)

    ready(0)
    step(0, 0, None, None)

    def two(g, _):
        t = g * 2
        ready(t + 1)
        ready_values(t)
        step(t + 1, 1, t, 0)
        returns(t)
        ready(t + 2)
        step(jnp.minimum(t + 2, 31), 0, t + 1, 1)
        returns(t + 1)
        return 0

    lax.fori_loop(0, 16, two, 0)

    relay_long(2)
    relay_short(2)
    relay_long(3)

    def ag_copy(slot, piece):
        i = slot * PIECES + piece
        rows = pl.ds(piece * PART, PART)
        to = 1 if rising(slot, piece) else -1
        return remote(mixed.at[before(slot, piece), rows], mixed.at[slot, rows], ag_send.at[i], ag_recv.at[i], z_at(to))

    def finish(piece, state):
        sums, total, _ = joined(state, piece, long_way(piece)[3])
        token = piece * PART + lax.broadcasted_iota(jnp.int32, (1, LANES), 1) // GROUP
        live = z * TOKENS + token < jnp.where(side == 0, len_ref[0], len_ref[1])
        done = jnp.where(live, sums / total, 0.0)
        turn[piece] = done.T
        for j in range(GROUP):
            mixed[0, pl.ds(piece * PART, PART), j * WIDTH:(j + 1) * WIDTH] = turn[piece, pl.ds(j, PART, stride=GROUP), :].astype(BF16)
        ag_copy(1, piece).start()
        ag_copy(2, piece).start()

    def arrive(*slots):
        for piece in range(PIECES):
            for slot in slots:
                ag_copy(slot, piece).wait_recv()
                for later in range(3, RING):
                    if before(later, piece) == slot:
                        ag_copy(later, piece).start()

    def chip_of(slot):
        return (z + (-((slot + 1) // 2) if slot % 2 == 1 else slot // 2) + RING) % RING

    def to_mate(slot, block):
        i = slot * 2 + block
        return remote(part.at[slot, block], mate_in.at[slot, block], co_send.at[i], co_recv.at[i], mate)

    def given(slot):
        return (chip_of(slot) // 2) % 2 != core

    def project(block, first, last):
        rows = mixed[first:last].reshape((last - first) * TOKENS, FEATURES)
        terms = jnp.dot(rows, w_all[block], preferred_element_type=F32)
        part[first:last, block] = terms.reshape(last - first, TOKENS, COLUMNS)

        for slot in range(first, last):
            @pl.when(given(slot))
            def _():
                to_mate(slot, block).start()

    def y_copy(block, far, which):
        i = (block * 2 + far) * 2 + which
        to = {"ctx": block * RING + z, "head": (2 * side + far) * 2 + core}
        return remote(y_out.at[i], y_in.at[y * 2 + which], y_send.at[i], y_recv.at[y * 2 + which], to)

    def stays(block, far):
        return jnp.logical_and(block == side, 2 * side + far == y)

    def spread(block, first, last):
        for slot in range(first, last):
            at = chip_of(slot)
            far, which = at // 4, at % 2

            @pl.when(jnp.logical_not(given(slot)))
            def _():
                to_mate(slot, block).wait_recv()
                both = part[slot, block] + mate_in[slot, block]

                @pl.when(stays(block, far))
                def _():
                    own[which] = both

                @pl.when(jnp.logical_not(stays(block, far)))
                def _():
                    y_out[(block * 2 + far) * 2 + which] = both.astype(BF16)
                    y_copy(block, far, which).start()

    there = 1 - side
    half_done = [joined(mine(0, piece), piece, short_way(piece)[2]) for piece in range(PIECES)]
    for piece in range(PIECES):
        finish(piece, half_done[piece])
    w_load.wait()
    arrive(1, 2)
    arrive(3, 4)
    project(side, 0, 3)
    arrive(5, 6)
    project(side, 3, 5)
    spread(side, 0, 3)
    w_copy.wait_recv()
    project(there, 0, 5)
    project(side, 5, 7)
    spread(there, 0, 5)
    project(there, 5, 7)
    spread(side, 3, 7)
    spread(there, 5, 7)
    arrive(7)
    project(there, 7, 8)
    project(side, 7, 8)
    spread(there, 7, 8)
    spread(side, 7, 8)

    def taken(source, which):
        i = source * 2 + which
        remote(y_out.at[which], y_in.at[i], y_send.at[which], y_recv.at[i], opposite(source)).wait_recv()
        return y_in[i].astype(F32)

    for which in range(2):
        rows = pl.ds(which * TOKENS, TOKENS)

        @pl.when(y // 2 == side)
        def _():
            out_ref[rows, :] = own[which] + taken((y + 1) % 4, which) + taken((y + 2) % 4, which) + taken((y + 3) % 4, which)

        @pl.when(y // 2 != side)
        def _():
            out_ref[rows, :] = taken(0, which) + taken(1, which) + taken(2, which) + taken(3, which)

    for index in range(4):
        kv_copy(index).wait_send()
    for slot in range(1, RING):
        for half in range(2):
            q_copy(None, half, slot).wait_send()
        for piece in range(PIECES):
            rs_copy(slot, piece).wait_send()
            ag_copy(slot, piece).wait_send()
    w_copy.wait_send()
    for slot in range(RING):
        @pl.when(given(slot))
        def _():
            for block in range(2):
                to_mate(slot, block).wait_send()
    for block in range(2):
        for far in range(2):
            for which in range(2):
                @pl.when(jnp.logical_not(stays(block, far)))
                def _():
                    y_copy(block, far, which).wait_send()


def body(queries, keys, values, lengths, prompt_lengths, out_weight):
    hbm = pl.BlockSpec(memory_space=pltpu.HBM)
    smem = pl.BlockSpec(memory_space=pltpu.SMEM)
    dma = pltpu.SemaphoreType.DMA
    return pl.pallas_call(
        kernel,
        out_shape=pltpu.VMEM((2 * TOKENS, COLUMNS), F32),
        in_specs=[hbm, hbm, hbm, smem, smem, hbm],
        out_specs=pl.BlockSpec(memory_space=pltpu.VMEM),
        scratch_shapes=[
            pltpu.VMEM((2 * SPAN, WIDTH), BF16),
            pltpu.VMEM((2, FEATURES, COLUMNS), BF16),
            pltpu.VMEM((RING, ROWS, WIDTH), BF16),
            pltpu.VMEM((4, SPAN, WIDTH), BF16),
            pltpu.VMEM((4, WIDTH + 16, SPAN), BF16),
            pltpu.VMEM((2, SPAN, ROWS), F32),
            pltpu.VMEM((2, 8, ROWS), F32),
            pltpu.VMEM((RING, WIDTH + 8, ROWS), F32),
            pltpu.VMEM((RING, 8, ROWS), F32),
            pltpu.VMEM((RING * PIECES, WIDTH + 16, LANES), BF16),
            pltpu.VMEM((RING * PIECES, WIDTH + 16, LANES), BF16),
            pltpu.VMEM((PIECES, LANES, WIDTH), F32),
            pltpu.VMEM((RING, TOKENS, FEATURES), BF16),
            pltpu.VMEM((RING, 2, TOKENS, COLUMNS), F32),
            pltpu.VMEM((RING, 2, TOKENS, COLUMNS), F32),
            pltpu.VMEM((8, TOKENS, COLUMNS), BF16),
            pltpu.VMEM((8, TOKENS, COLUMNS), BF16),
            pltpu.VMEM((2, TOKENS, COLUMNS), F32),
            dma((5,)),
            dma((4,)), dma((4,)),
            dma((2 * RING,)), dma((2 * RING,)),
            dma((RING * PIECES,)), dma((RING * PIECES,)),
            dma, dma,
            dma((RING * PIECES,)), dma((RING * PIECES,)),
            dma((2 * RING,)), dma((2 * RING,)),
            dma((8,)), dma((8,)),
        ],
        compiler_params=pltpu.CompilerParams(
            collective_id=1, has_side_effects=True, vmem_limit_bytes=56 << 20
        ),
        name="paired_attention",
    )(
        queries.reshape(ROWS, WIDTH),
        keys.reshape(2 * SPAN, WIDTH),
        values.reshape(2 * SPAN, WIDTH),
        lengths,
        prompt_lengths,
        out_weight,
    )


def solution(mesh):
    in_specs = (
        P(("pair", "ctx"), "head", None),
        P(("pair", "ctx"), "head", None),
        P(("pair", "ctx"), "head", None),
        P("pair"),
        P("pair"),
        P("head", "ctx"),
    )
    out_specs = P(("pair", "head"), "ctx")
    return jax.shard_map(body, mesh=mesh, in_specs=in_specs, out_specs=out_specs, check_vma=False)
```
